32 devices in a mesh: dp: 2 (over y), row: 4 (over z), col: 4 (over x, core).
Axes of the slice: x: 2, y: 2, z: 4, core: 2. Of those that a mesh axis runs over, the one named last changes fastest.
Arguments:
- tokens: bfloat16 [8192, 1152], P(('dp', 'col'), 'row'), may hold values from -1 to 3
- class_ids: int32 [8], P('dp'), may hold values from 0 to 999
- time_ids: int32 [8], P('dp'), may hold values from 0 to 999
- class_table: bfloat16 [1000, 1152], P(None, 'col'), may hold values from -6 to 6
- adaptive_norm_weight: bfloat16 [1152, 6, 1152], P('col', None, 'row'), may hold values from -0.1875 to 0.1875
- adaptive_norm_bias: bfloat16 [6, 1152], P(None, 'row'), may hold values from -3 to 3
- query_key_value_weight: bfloat16 [1152, 3, 1152], P('row', None, 'col'), may hold values from -0.1875 to 0.1875
- query_value_bias: bfloat16 [2, 1152], P(None, 'col'), may hold values from -3 to 3
- w_out: bfloat16 [1152, 1152], P('col', 'row'), may hold values from -1.5 to 1.5
- out_bias: bfloat16 [1152], P('row'), may hold values from -3 to 3
- w_fc1: bfloat16 [1152, 4608], P('row', 'col'), may hold values from -0.1875 to 0.1875
- fc1_bias: bfloat16 [4608], P('col'), may hold values from -3 to 3
- w_fc2: bfloat16 [4608, 1152], P('col', 'row'), may hold values from -0.09375 to 0.09375
- fc2_bias: bfloat16 [1152], P('row'), may hold values from -3 to 3
- cotangent: bfloat16 [8192, 1152], P(('dp', 'col'), 'row'), may hold values from -6 to 6
Outputs:
- mixed: bfloat16 [8192, 1152], P(('dp', 'col'), 'row')
- d_tokens: float32 [8192, 1152], P(('dp', 'col'), 'row')
- d_class_table: float32 [1000, 1152], P(None, 'col')
- d_ada_weight: float32 [1152, 6, 1152], P('col', None, 'row')
- d_ada_bias: float32 [6, 1152], P(None, 'row')
- d_w_qkv: float32 [1152, 3, 1152], P('row', None, 'col')
- d_query_value_bias: float32 [2, 1152], P(None, 'col')
- d_w_out: float32 [1152, 1152], P('col', 'row')
- d_out_bias: float32 [1152], P('row')
- d_w_fc1: float32 [1152, 4608], P('row', 'col')
- d_fc1_bias: float32 [4608], P('col')
- d_w_fc2: float32 [4608, 1152], P('col', 'row')
- d_fc2_bias: float32 [1152], P('row')
The draws below stay inside these ranges and needn't reach their ends.
All inputs are finite; a program needn't handle non-finite values.
Results may differ from the reference program's by a relative error of at most 0.014.
The reference program's roundings to bfloat16 on the way count: a program that leaves them out, or rounds other values in their place, can miss the bound.
Values may be sent and summed in bfloat16 or wider, within the bound.
A program may use at most 192 MiB of HBM per device.

```python
import math
import jax
import jax.numpy as jnp
from jax import lax

D = 1152
HEADS = 16
HD = 72
FF = 4608
NCLS = 1000
NSTEPS = 1000
SEQ = 1024
LATENTS = 8
TOKENS = 8192


def touch_ends(entries, rng, least, largest):
    dims = entries.shape
    index_at = [jax.random.randint(jax.random.fold_in(rng, axis), (), 0, dims[axis]) for axis in range(len(dims))]
    entries = entries.at[tuple(index_at)].set(least)
    longest = dims.index(max(dims))
    index_at[longest] = (index_at[longest] + 1) % dims[longest]
    return entries.at[tuple(index_at)].set(largest)


def steps_of(stream_key, shape, pieces, least, largest):
    factor_of = 1.0
    for dim, parts in pieces:
        heights = jax.random.uniform(jax.random.fold_in(jax.random.fold_in(stream_key, 6), dim), (parts,), jnp.float32, least / len(pieces), largest / len(pieces))
        factor_of = factor_of * jnp.repeat(jnp.exp(heights), shape[dim] // parts).reshape((-1,) + (1,) * (len(shape) - 1 - dim))
    return factor_of


def scatter_about(key, dims, width, bound, cuts=(), kind=jnp.bfloat16):
    entries = jax.random.normal(key, dims, jnp.float32) * width
    if len(cuts) > 0:
        entries = steps_of(key, dims, cuts, -0.22, 0.18) * entries
    return jnp.clip(entries, min=-bound, max=bound).astype(kind)


def setup_inputs(seed: int = 0) -> dict:
    key_list = jax.random.split(jax.random.key(seed), 16)
    tokens = jnp.clip(-1.0 + 4.0 * jax.random.uniform(key_list[0], (TOKENS, D), jnp.float32) ** steps_of(key_list[0], (TOKENS, D), ((0, 8), (1, 4)), -0.2, 0.2), -1.0, 3.0).astype(jnp.bfloat16)
    class_ids = touch_ends(jax.random.randint(key_list[1], (LATENTS,), 0, NCLS), jax.random.fold_in(key_list[1], 1), 0, NCLS - 1).astype(jnp.int32)
    time_ids = touch_ends(jax.random.randint(key_list[2], (LATENTS,), 0, NSTEPS), jax.random.fold_in(key_list[2], 1), 0, NSTEPS - 1).astype(jnp.int32)
    class_table = scatter_about(key_list[3], (NCLS, D), 1.0, 6.0, ((1, 4),))
    adaptive_norm_weight = scatter_about(key_list[4], (D, 6, D), D ** -0.5, 0.1875, ((0, 4), (2, 4)))
    adaptive_norm_bias = scatter_about(key_list[5], (6, D), 0.5, 3.0, ((1, 4),))
    query_key_value_weight = scatter_about(key_list[6], (D, 3, D), D ** -0.5, 0.1875, ((0, 4), (2, 4)))
    query_value_bias = scatter_about(key_list[7], (2, D), 0.5, 3.0, ((1, 4),))
    w_out = scatter_about(key_list[8], (D, D), (D // 64) ** -0.5, 1.5, ((0, 4), (1, 4)))
    out_bias = scatter_about(key_list[9], (D,), 0.5, 3.0, ((0, 4),))
    w_fc1 = scatter_about(key_list[10], (D, FF), D ** -0.5, 0.1875, ((0, 4), (1, 4)))
    fc1_bias = scatter_about(key_list[11], (FF,), 0.5, 3.0, ((0, 4),))
    w_fc2 = scatter_about(key_list[12], (FF, D), FF ** -0.5, 0.09375, ((0, 4), (1, 4)))
    fc2_bias = scatter_about(key_list[13], (D,), 0.5, 3.0, ((0, 4),))
    cotangent = scatter_about(key_list[14], (TOKENS, D), 1.0, 6.0, ((0, 8), (1, 4)))
    return {"tokens": tokens, "class_ids": class_ids, "time_ids": time_ids, "class_table": class_table, "adaptive_norm_weight": adaptive_norm_weight, "adaptive_norm_bias": adaptive_norm_bias, "query_key_value_weight": query_key_value_weight, "query_value_bias": query_value_bias, "w_out": w_out, "out_bias": out_bias, "w_fc1": w_fc1, "fc1_bias": fc1_bias, "w_fc2": w_fc2, "fc2_bias": fc2_bias, "cotangent": cotangent}


@jax.custom_vjp
def low(v):
    return lax.optimization_barrier(v.astype(jnp.bfloat16)).astype(jnp.float32)

@jax.custom_vjp
def low_back(v):
    return v

def low_keep(v):
    return (low(v), None)

def low_pass(kept, grad):
    return (grad,)

def back_keep(v):
    return (v, None)

def back_low(kept, grad):
    return (low(grad),)
low.defvjp(low_keep, low_pass)
low_back.defvjp(back_keep, back_low)

def time_embedding(time_ids):
    half_width = D // 2
    freqs = jnp.exp(-math.log(10000.0) * jnp.arange(half_width, dtype=jnp.float32) / half_width)
    angles = time_ids.astype(jnp.float32)[:, None] * freqs[None, :]
    return jnp.concatenate([jnp.cos(angles), jnp.sin(angles)], axis=-1)

def layer_norm(values):
    center = lax.optimization_barrier(jnp.mean(values, axis=-1, keepdims=True))
    centred = values - center
    spread = lax.optimization_barrier(jnp.mean(centred * centred, axis=-1, keepdims=True))
    return centred * lax.rsqrt(spread + 1e-06)

def attend(triple):
    queries, keys, values = triple
    highest_precision = lax.Precision.HIGHEST
    scores = low_back(jnp.einsum('qhe,khe->hqk', queries, keys, precision=highest_precision) / math.sqrt(HD))
    weights = low(jax.nn.softmax(scores, axis=-1))
    return jnp.einsum('hqk,khe->qhe', weights, values, precision=highest_precision).reshape(SEQ, D)

def block_forward(class_ids, time_ids, tokens, class_table, adaptive_norm_weight, adaptive_norm_bias, query_key_value_weight, query_value_bias, w_out, out_bias, w_fc1, fc1_bias, w_fc2, fc2_bias):
    highest_precision = lax.Precision.HIGHEST
    condition = class_table[class_ids] + time_embedding(time_ids)
    silu_condition = low(jax.nn.silu(condition))
    modulation_vectors = jnp.einsum('au,uop->aop', silu_condition, adaptive_norm_weight, precision=highest_precision) + adaptive_norm_bias[None]

    def rows_of(index):
        return modulation_vectors[:, index][:, None, :]
    latent_tokens = tokens.reshape(LATENTS, SEQ, D)
    residual_input_first = low(layer_norm(latent_tokens) * (1.0 + rows_of(1)) + rows_of(0)).reshape(TOKENS, D)
    bias_broadcast_rows = jnp.stack([query_value_bias[0], jnp.zeros_like(query_value_bias[0]), query_value_bias[1]])
    projected_condition = jnp.einsum('mw,wpx->mpx', residual_input_first, query_key_value_weight, precision=highest_precision) + bias_broadcast_rows[None]
    projected_condition = low(low_back(projected_condition))
    split = projected_condition.reshape(LATENTS, SEQ, 3, HEADS, HD)
    attended = lax.map(jax.checkpoint(attend), (split[:, :, 0], split[:, :, 1], split[:, :, 2]))
    attended = low(low_back(attended.reshape(TOKENS, D)))
    branch = low_back(jnp.dot(attended, w_out, precision=highest_precision) + out_bias)
    middle = latent_tokens + rows_of(2) * branch.reshape(LATENTS, SEQ, D)
    second_input = low(layer_norm(middle) * (1.0 + rows_of(4)) + rows_of(3)).reshape(TOKENS, D)
    hidden = low_back(jnp.dot(second_input, w_fc1, precision=highest_precision) + fc1_bias)
    activ = low(jax.nn.gelu(hidden, approximate=True))
    feed = low_back(jnp.dot(activ, w_fc2, precision=highest_precision) + fc2_bias)
    mixed = middle + rows_of(5) * feed.reshape(LATENTS, SEQ, D)
    return mixed.reshape(TOKENS, D)

def reference(tokens, class_ids, time_ids, class_table, adaptive_norm_weight, adaptive_norm_bias, query_key_value_weight, query_value_bias, w_out, out_bias, w_fc1, fc1_bias, w_fc2, fc2_bias, cotangent):

    def forward(*params):
        return block_forward(class_ids, time_ids, *params)
    floats = tuple((item.astype(jnp.float32) for item in (tokens, class_table, adaptive_norm_weight, adaptive_norm_bias, query_key_value_weight, query_value_bias, w_out, out_bias, w_fc1, fc1_bias, w_fc2, fc2_bias)))
    result, pullback = jax.vjp(forward, *floats)
    grads = pullback(cotangent.astype(jnp.float32))
    return (result.astype(jnp.bfloat16), grads[0], grads[1], grads[2], grads[3], grads[4], grads[5], grads[6], grads[7], grads[8], grads[9], grads[10], grads[11])
```

```python
from functools import partial
import math

import jax
import jax.numpy as jnp
from jax import lax
from jax.sharding import PartitionSpec as P

D = 1152
HD = 72
NCLS = 1000
SEQ = 1024


def time_embedding(time_ids):
    half_width = D // 2
    freqs = jnp.exp(-math.log(10000.0) * jnp.arange(half_width, dtype=jnp.float32) / half_width)
    angles = time_ids.astype(jnp.float32)[:, None] * freqs[None, :]
    return jnp.concatenate([jnp.cos(angles), jnp.sin(angles)], axis=-1)


def matmul(left, right, left_dim=1, right_dim=0):
    return lax.dot_general(
        left, right, (((left_dim,), (right_dim,)), ((), ())), preferred_element_type=jnp.float32
    )


def transposed(value):
    side = lax.axis_size("col")
    pairs = [(i * side + j, j * side + i) for i in range(side) for j in range(side)]
    return lax.ppermute(value, ("row", "col"), pairs)


def side_by_side(pieces):
    return jnp.concatenate([pieces[i] for i in range(pieces.shape[0])], axis=-1)


def gather_wide(value, axis_name):
    return side_by_side(lax.all_gather(value, axis_name, axis=0))


def in_blocks(wide, count):
    return jnp.stack(jnp.split(wide, count, axis=-1), axis=0)


def sum_scatter(blocks, axis_name):
    return lax.psum_scatter(
        blocks.astype(jnp.bfloat16), axis_name, scatter_dimension=0, tiled=False
    ).astype(jnp.float32)


def grad_sum(blocks):
    piece = lax.psum_scatter(
        blocks.astype(jnp.bfloat16), "row", scatter_dimension=0, tiled=False
    )
    both = lax.all_gather(piece, "dp", axis=0).astype(jnp.float32)
    return jnp.sum(both, axis=0)


def moments(values):
    mean = jnp.mean(values, axis=-1, keepdims=True)
    centred = values - mean
    spread = jnp.mean(centred * centred, axis=-1, keepdims=True)
    return mean, lax.rsqrt(spread + 1e-06)


def attend(queries, keys, values):
    scores = jnp.einsum("qhe,khe->hqk", queries, keys, preferred_element_type=jnp.float32) * (
        1.0 / math.sqrt(HD)
    )
    biggest = jnp.max(scores, axis=-1, keepdims=True)
    expo = jnp.exp(scores - biggest)
    totals = jnp.sum(expo, axis=-1, keepdims=True)
    weights = (expo / totals).astype(jnp.bfloat16)
    result = jnp.einsum("hqk,khe->qhe", weights, values, preferred_element_type=jnp.float32)
    return (result.reshape(SEQ, -1), (biggest + jnp.log(totals))[..., 0])


def attend_back(queries, keys, values, log_totals, d_result):
    scale = 1.0 / math.sqrt(HD)
    scores = jnp.einsum("qhe,khe->hqk", queries, keys, preferred_element_type=jnp.float32) * scale
    probs = jnp.exp(scores - log_totals[..., None])
    d_values = jnp.einsum(
        "hqk,qhe->khe", probs.astype(jnp.bfloat16), d_result, preferred_element_type=jnp.float32
    )
    d_probs = jnp.einsum("qhe,khe->hqk", d_result, values, preferred_element_type=jnp.float32)
    inner = jnp.sum(probs * d_probs, axis=-1, keepdims=True)
    d_scores = (probs * (d_probs - inner)).astype(jnp.bfloat16)
    d_queries = (
        jnp.einsum("hqk,khe->qhe", d_scores, keys, preferred_element_type=jnp.float32) * scale
    )
    d_keys = (
        jnp.einsum("hqk,qhe->khe", d_scores, queries, preferred_element_type=jnp.float32) * scale
    )
    return jnp.concatenate(
        [d_queries.reshape(SEQ, -1), d_keys.reshape(SEQ, -1), d_values.reshape(SEQ, -1)], axis=1
    ).astype(jnp.bfloat16)


def norm_back(d_input, scale_row, normed, inv_std, sums):
    d_normed = d_input * (1.0 + scale_row)
    return inv_std * (d_normed - sums[0][:, None] / D - normed * sums[1][:, None] / D)


def norm_sums(partial_input, scale_row, normed):
    d_normed = partial_input * (1.0 + scale_row)
    return lax.psum(
        jnp.stack([jnp.sum(d_normed, axis=-1), jnp.sum(d_normed * normed, axis=-1)]), "col"
    )


def per_device(
    tokens,
    class_ids,
    time_ids,
    class_table,
    adaptive_norm_weight,
    adaptive_norm_bias,
    query_key_value_weight,
    query_value_bias,
    w_out,
    out_bias,
    w_fc1,
    fc1_bias,
    w_fc2,
    fc2_bias,
    cotangent,
):
    highest = lax.Precision.HIGHEST
    f32 = jnp.float32
    bf16 = jnp.bfloat16
    rows, cols = lax.axis_size("row"), lax.axis_size("col")
    row, col = lax.axis_index("row"), lax.axis_index("col")
    width = class_table.shape[1]
    heads_here = width // HD
    local_lats = class_ids.shape[0]
    assert rows == cols == local_lats and tokens.shape[0] == SEQ

    tok_block = transposed(tokens)
    tok = gather_wide(tok_block, "col").astype(f32)
    tok_block = tok_block.astype(f32)
    dy_block = transposed(cotangent)
    dy = gather_wide(dy_block, "col").astype(f32)
    dy_block = dy_block.astype(f32)

    w_qkv = query_key_value_weight.reshape(width, 3 * width)
    w_qkv_all = lax.all_gather(w_qkv, "row", axis=0, tiled=True)
    w_out_here = gather_wide(w_out, "row")
    w_out_all = lax.all_gather(w_out_here, "col", axis=0, tiled=True)
    w_fc1_all = lax.all_gather(w_fc1, "row", axis=0, tiled=True)
    w_fc2_all = gather_wide(w_fc2, "row")

    def embed(labels, steps):
        onehot = (labels[:, None] == jnp.arange(NCLS, dtype=jnp.int32)[None, :]).astype(bf16)
        timing = lax.dynamic_slice_in_dim(time_embedding(steps), col * width, width, 1)
        return onehot, jnp.dot(onehot, class_table, preferred_element_type=f32) + timing

    here = jax.nn.silu(embed(class_ids, time_ids)[1]).astype(bf16)
    pieces = jnp.einsum("au,uop->aop", here, adaptive_norm_weight, preferred_element_type=f32)
    pieces = pieces + jnp.where(col == 0, 1.0, 0.0) * adaptive_norm_bias.astype(f32)[None]
    packed = jnp.concatenate(
        [
            pieces.reshape(local_lats * 6, width),
            out_bias.astype(f32)[None],
            fc2_bias.astype(f32)[None],
        ],
        axis=0,
    )
    packed = lax.all_gather(packed, ("row", "col"), axis=0).reshape(rows, cols, -1, width)
    mod_blocks = jnp.sum(
        lax.dynamic_slice_in_dim(packed, row * 6, 6, 2), axis=1
    )
    mod_here = lax.dynamic_index_in_dim(mod_blocks, col, 0, keepdims=False)
    mod = side_by_side(mod_blocks)
    bias_blocks = packed[:, 0, local_lats * 6 :]
    bias_here = lax.dynamic_index_in_dim(bias_blocks, col, 0, keepdims=False)
    out_bias_all = side_by_side(bias_blocks)[0]

    mean1, inv1 = moments(tok)
    normed1 = (tok - mean1) * inv1
    input1 = (normed1 * (1.0 + mod[1]) + mod[0]).astype(bf16)
    qv_bias = query_value_bias.astype(f32)
    qkv_bias = jnp.concatenate([qv_bias[0], jnp.zeros_like(qv_bias[0]), qv_bias[1]])
    qkv = (matmul(input1, w_qkv_all) + qkv_bias).astype(bf16)
    split = qkv.reshape(SEQ, 3, heads_here, HD)
    queries, keys, values = (split[:, 0], split[:, 1], split[:, 2])
    attended, log_totals = attend(queries, keys, values)
    attended = attended.astype(bf16)
    attended_all = gather_wide(attended, "col")
    branch = matmul(attended_all, w_out_all) + out_bias_all
    middle = tok + mod[2] * branch
    mean2, inv2 = moments(middle)
    normed2 = (middle - mean2) * inv2
    input2 = (normed2 * (1.0 + mod[4]) + mod[3]).astype(bf16)
    branch_here = lax.dynamic_slice_in_dim(branch, col * width, width, 1)
    middle_here = tok_block + mod_here[2] * branch_here
    normed2_here = (middle_here - mean2) * inv2
    normed1_here = (tok_block - mean1) * inv1

    hidden = matmul(input2, w_fc1_all) + fc1_bias.astype(f32)
    gelu_fn = partial(jax.nn.gelu, approximate=True)
    activ = gelu_fn(hidden).astype(bf16)
    feed = sum_scatter(in_blocks(matmul(activ, w_fc2_all), cols), "col") + bias_here[1]
    mixed = transposed((middle_here + mod_here[5] * feed).astype(bf16))

    d_feed = (dy * mod[5]).astype(bf16)
    d_hidden = jax.vjp(gelu_fn, hidden)[1](matmul(d_feed, w_fc2_all, 1, 1))[0].astype(bf16)
    d_input2 = matmul(d_hidden, w_fc1_all, 1, 1)
    sums2 = norm_sums(d_input2, mod[4], normed2)
    d_input2 = sum_scatter(in_blocks(d_input2, cols), "col")
    d_w_fc2 = grad_sum(in_blocks(matmul(activ, d_feed, 0, 0), rows))
    d_w_fc1 = grad_sum(matmul(input2, d_hidden, 0, 0).reshape(rows, width, -1))
    d_fc1_bias = jnp.sum(d_hidden.astype(f32), axis=0)
    d_fc2_bias = jnp.sum((dy_block * mod_here[5]).astype(bf16).astype(f32), axis=0)
    d_middle = dy_block + norm_back(d_input2, mod_here[4], normed2_here, inv2, sums2)
    d_branch_here = (d_middle * mod_here[2]).astype(bf16)
    d_branch = gather_wide(d_branch_here, "col")
    d_attended = matmul(d_branch, w_out_here, 1, 1).astype(bf16).reshape(SEQ, heads_here, HD)
    d_w_out = grad_sum(in_blocks(matmul(attended, d_branch, 0, 0), rows))
    d_out_bias = jnp.sum(d_branch_here.astype(f32), axis=0)

    early = jnp.stack(
        [
            jnp.sum(d_middle * branch_here, axis=0),
            jnp.sum(d_input2, axis=0),
            jnp.sum(d_input2 * normed2_here, axis=0),
            jnp.sum(dy_block * feed, axis=0),
            d_out_bias,
            d_fc2_bias,
        ]
    )

    d_qkv = attend_back(queries, keys, values, log_totals, d_attended)
    d_input1 = matmul(d_qkv, w_qkv_all, 1, 1)
    sums1 = norm_sums(d_input1, mod[1], normed1)
    d_input1 = sum_scatter(in_blocks(d_input1, cols), "col")
    d_w_qkv = grad_sum(matmul(input1, d_qkv, 0, 0).reshape(rows, width, 3 * width))
    d_w_qkv = d_w_qkv.reshape(width, 3, width)
    d_qkv_sums = jnp.sum(d_qkv.astype(f32), axis=0).reshape(3, width)
    d_tokens = d_middle + norm_back(d_input1, mod_here[1], normed1_here, inv1, sums1)
    d_tokens = transposed(d_tokens.astype(bf16)).astype(f32)

    late = jnp.stack([jnp.sum(d_input1, axis=0), jnp.sum(d_input1 * normed1_here, axis=0)])

    def every_latent(part):
        full = lax.all_gather(part, ("dp", "row", "col"), axis=0)
        full = full.reshape(-1, cols, part.shape[0], width)
        return lax.dynamic_index_in_dim(full, row, 1, keepdims=False)

    early, late = every_latent(early), every_latent(late)
    d_out_bias = jnp.sum(early[:, 4], axis=0)
    d_fc2_bias = jnp.sum(early[:, 5], axis=0)
    d_mod = jnp.concatenate([late, early[:, :4]], axis=1)
    d_ada_bias = jnp.sum(d_mod, axis=0)
    all_ids = lax.all_gather(jnp.stack([class_ids, time_ids]), "dp", axis=1, tiled=True)
    onehot, condition = embed(all_ids[0], all_ids[1])
    activated = jax.nn.silu(condition).astype(bf16).astype(f32)
    d_ada_weight = jnp.einsum("qk,qfb->kfb", activated, d_mod, precision=highest)
    d_activated = jnp.einsum(
        "qnp,unp->qu", d_mod, adaptive_norm_weight.astype(f32), precision=highest
    )
    d_activated = lax.psum(d_activated, "row")
    d_condition = jax.vjp(jax.nn.silu, condition)[1](d_activated)[0]
    d_table = lax.dot_general(
        onehot.astype(f32), d_condition, (((0,), (0,)), ((), ())), precision=highest
    )
    bias_sums = lax.psum(
        jnp.concatenate([d_fc1_bias, d_qkv_sums[0], d_qkv_sums[2]]), ("dp", "row")
    )
    d_fc1_bias = bias_sums[: d_fc1_bias.shape[0]]
    d_query_value_bias = bias_sums[d_fc1_bias.shape[0] :].reshape(2, width)
    return (
        mixed,
        d_tokens,
        d_table,
        d_ada_weight,
        d_ada_bias,
        d_w_qkv,
        d_query_value_bias,
        d_w_out,
        d_out_bias,
        d_w_fc1,
        d_fc1_bias,
        d_w_fc2,
        d_fc2_bias,
    )


def solution(mesh):
    return jax.shard_map(
        per_device,
        mesh=mesh,
        in_specs=(
            P(("dp", "col"), "row"),
            P("dp"),
            P("dp"),
            P(None, "col"),
            P("col", None, "row"),
            P(None, "row"),
            P("row", None, "col"),
            P(None, "col"),
            P("col", "row"),
            P("row"),
            P("row", "col"),
            P("col"),
            P("col", "row"),
            P("row"),
            P(("dp", "col"), "row"),
        ),
        out_specs=(
            P(("dp", "col"), "row"),
            P(("dp", "col"), "row"),
            P(None, "col"),
            P("col", None, "row"),
            P(None, "row"),
            P("row", None, "col"),
            P(None, "col"),
            P("col", "row"),
            P("row"),
            P("row", "col"),
            P("col"),
            P("col", "row"),
            P("row"),
        ),
        check_vma=False,
    )
```

```python
from functools import partial
import math

import jax
import jax.numpy as jnp
from jax import lax
from jax.sharding import PartitionSpec as P

D = 1152
HD = 72
NCLS = 1000
SEQ = 1024


def time_embedding(time_ids):
    half_width = D // 2
    freqs = jnp.exp(-math.log(10000.0) * jnp.arange(half_width, dtype=jnp.float32) / half_width)
    angles = time_ids.astype(jnp.float32)[:, None] * freqs[None, :]
    return jnp.concatenate([jnp.cos(angles), jnp.sin(angles)], axis=-1)


def matmul(left, right, left_dim=1, right_dim=0):
    return lax.dot_general(
        left, right, (((left_dim,), (right_dim,)), ((), ())), preferred_element_type=jnp.float32
    )


def transposed(value):
    side = lax.axis_size("col")
    pairs = [(i * side + j, j * side + i) for i in range(side) for j in range(side)]
    return lax.ppermute(value, ("row", "col"), pairs)


def side_by_side(pieces):
    return jnp.concatenate([pieces[i] for i in range(pieces.shape[0])], axis=-1)


def gather_wide(value, axis_name):
    return side_by_side(lax.all_gather(value, axis_name, axis=0))


def in_blocks(wide, count):
    return jnp.stack(jnp.split(wide, count, axis=-1), axis=0)


def sum_scatter(blocks, axis_name):
    return lax.psum_scatter(
        blocks.astype(jnp.bfloat16), axis_name, scatter_dimension=0, tiled=False
    ).astype(jnp.float32)


def grad_sum(blocks):
    piece = lax.psum_scatter(
        blocks.astype(jnp.bfloat16), "row", scatter_dimension=0, tiled=False
    )
    if lax.axis_size("dp") == 2:
        other = lax.ppermute(piece, "dp", [(0, 1), (1, 0)])
        return piece.astype(jnp.float32) + other.astype(jnp.float32)
    both = lax.all_gather(piece, "dp", axis=0).astype(jnp.float32)
    return jnp.sum(both, axis=0)


def moments(values):
    mean = jnp.mean(values, axis=-1, keepdims=True)
    centred = values - mean
    spread = jnp.mean(centred * centred, axis=-1, keepdims=True)
    return mean, lax.rsqrt(spread + 1e-06)


def attend(queries, keys, values):
    scores = jnp.einsum("qhe,khe->hqk", queries, keys, preferred_element_type=jnp.float32) * (
        1.0 / math.sqrt(HD)
    )
    biggest = jnp.max(scores, axis=-1, keepdims=True)
    expo = jnp.exp(scores - biggest)
    totals = jnp.sum(expo, axis=-1, keepdims=True)
    weights = (expo / totals).astype(jnp.bfloat16)
    result = jnp.einsum("hqk,khe->qhe", weights, values, preferred_element_type=jnp.float32)
    return (result.reshape(SEQ, -1), (biggest + jnp.log(totals))[..., 0])


def attend_back(queries, keys, values, log_totals, d_result):
    scale = 1.0 / math.sqrt(HD)
    scores = jnp.einsum("qhe,khe->hqk", queries, keys, preferred_element_type=jnp.float32) * scale
    probs = jnp.exp(scores - log_totals[..., None])
    d_values = jnp.einsum(
        "hqk,qhe->khe", probs.astype(jnp.bfloat16), d_result, preferred_element_type=jnp.float32
    )
    d_probs = jnp.einsum("qhe,khe->hqk", d_result, values, preferred_element_type=jnp.float32)
    inner = jnp.sum(probs * d_probs, axis=-1, keepdims=True)
    d_scores = (probs * (d_probs - inner)).astype(jnp.bfloat16)
    d_queries = (
        jnp.einsum("hqk,khe->qhe", d_scores, keys, preferred_element_type=jnp.float32) * scale
    )
    d_keys = (
        jnp.einsum("hqk,qhe->khe", d_scores, queries, preferred_element_type=jnp.float32) * scale
    )
    return jnp.concatenate(
        [d_queries.reshape(SEQ, -1), d_keys.reshape(SEQ, -1), d_values.reshape(SEQ, -1)], axis=1
    ).astype(jnp.bfloat16)


def norm_back(d_input, scale_row, normed, inv_std, sums):
    d_normed = d_input * (1.0 + scale_row)
    return inv_std * (d_normed - sums[0][:, None] / D - normed * sums[1][:, None] / D)


def norm_sums(partial_input, scale_row, normed):
    d_normed = partial_input * (1.0 + scale_row)
    return lax.psum(
        jnp.stack([jnp.sum(d_normed, axis=-1), jnp.sum(d_normed * normed, axis=-1)]), "col"
    )


def per_device(
    tokens,
    class_ids,
    time_ids,
    class_table,
    adaptive_norm_weight,
    adaptive_norm_bias,
    query_key_value_weight,
    query_value_bias,
    w_out,
    out_bias,
    w_fc1,
    fc1_bias,
    w_fc2,
    fc2_bias,
    cotangent,
):
    highest = lax.Precision.HIGHEST
    f32 = jnp.float32
    bf16 = jnp.bfloat16
    rows, cols = lax.axis_size("row"), lax.axis_size("col")
    row, col = lax.axis_index("row"), lax.axis_index("col")
    width = class_table.shape[1]
    heads_here = width // HD
    local_lats = class_ids.shape[0]
    assert rows == cols == local_lats and tokens.shape[0] == SEQ

    tok_block = transposed(tokens)
    tok = gather_wide(tok_block, "col").astype(f32)
    tok_block = tok_block.astype(f32)
    dy_block = transposed(cotangent)
    dy = gather_wide(dy_block, "col").astype(f32)
    dy_block = dy_block.astype(f32)

    w_qkv = query_key_value_weight.reshape(width, 3 * width)
    w_qkv_all = lax.all_gather(w_qkv, "row", axis=0, tiled=True)
    w_out_here = gather_wide(w_out, "row")
    w_out_all = lax.all_gather(w_out_here, "col", axis=0, tiled=True)
    w_fc1_all = lax.all_gather(w_fc1, "row", axis=0, tiled=True)
    w_fc2_all = gather_wide(w_fc2, "row")

    def embed(labels, steps):
        onehot = (labels[:, None] == jnp.arange(NCLS, dtype=jnp.int32)[None, :]).astype(bf16)
        timing = lax.dynamic_slice_in_dim(time_embedding(steps), col * width, width, 1)
        return onehot, jnp.dot(onehot, class_table, preferred_element_type=f32) + timing

    here = jax.nn.silu(embed(class_ids, time_ids)[1]).astype(bf16)
    pieces = jnp.einsum("au,uop->aop", here, adaptive_norm_weight, preferred_element_type=f32)
    pieces = pieces + jnp.where(col == 0, 1.0, 0.0) * adaptive_norm_bias.astype(f32)[None]
    packed = jnp.concatenate(
        [
            pieces.reshape(local_lats * 6, width),
            out_bias.astype(f32)[None],
            fc2_bias.astype(f32)[None],
        ],
        axis=0,
    )
    packed = lax.all_gather(packed, ("row", "col"), axis=0).reshape(rows, cols, -1, width)
    mod_blocks = jnp.sum(
        lax.dynamic_slice_in_dim(packed, row * 6, 6, 2), axis=1
    )
    mod_here = lax.dynamic_index_in_dim(mod_blocks, col, 0, keepdims=False)
    mod = side_by_side(mod_blocks)
    bias_blocks = packed[:, 0, local_lats * 6 :]
    bias_here = lax.dynamic_index_in_dim(bias_blocks, col, 0, keepdims=False)
    out_bias_all = side_by_side(bias_blocks)[0]

    mean1, inv1 = moments(tok)
    normed1 = (tok - mean1) * inv1
    input1 = (normed1 * (1.0 + mod[1]) + mod[0]).astype(bf16)
    qv_bias = query_value_bias.astype(f32)
    qkv_bias = jnp.concatenate([qv_bias[0], jnp.zeros_like(qv_bias[0]), qv_bias[1]])
    qkv = (matmul(input1, w_qkv_all) + qkv_bias).astype(bf16)
    split = qkv.reshape(SEQ, 3, heads_here, HD)
    queries, keys, values = (split[:, 0], split[:, 1], split[:, 2])
    attended, log_totals = attend(queries, keys, values)
    attended = attended.astype(bf16)
    attended_all = gather_wide(attended, "col")
    branch = matmul(attended_all, w_out_all) + out_bias_all
    middle = tok + mod[2] * branch
    mean2, inv2 = moments(middle)
    normed2 = (middle - mean2) * inv2
    input2 = (normed2 * (1.0 + mod[4]) + mod[3]).astype(bf16)
    branch_here = lax.dynamic_slice_in_dim(branch, col * width, width, 1)
    middle_here = tok_block + mod_here[2] * branch_here
    normed2_here = (middle_here - mean2) * inv2
    normed1_here = (tok_block - mean1) * inv1

    hidden = matmul(input2, w_fc1_all) + fc1_bias.astype(f32)
    gelu_fn = partial(jax.nn.gelu, approximate=True)
    activ = gelu_fn(hidden).astype(bf16)
    feed = sum_scatter(in_blocks(matmul(activ, w_fc2_all), cols), "col") + bias_here[1]
    mixed = transposed((middle_here + mod_here[5] * feed).astype(bf16))

    d_feed = (dy * mod[5]).astype(bf16)
    d_hidden = jax.vjp(gelu_fn, hidden)[1](matmul(d_feed, w_fc2_all, 1, 1))[0].astype(bf16)
    d_input2 = matmul(d_hidden, w_fc1_all, 1, 1)
    sums2 = norm_sums(d_input2, mod[4], normed2)
    d_input2 = sum_scatter(in_blocks(d_input2, cols), "col")
    d_w_fc2 = grad_sum(in_blocks(matmul(activ, d_feed, 0, 0), rows))
    d_w_fc1 = grad_sum(matmul(input2, d_hidden, 0, 0).reshape(rows, width, -1))
    d_fc1_bias = jnp.sum(d_hidden.astype(f32), axis=0)
    d_fc2_bias = jnp.sum((dy_block * mod_here[5]).astype(bf16).astype(f32), axis=0)
    d_middle = dy_block + norm_back(d_input2, mod_here[4], normed2_here, inv2, sums2)
    d_branch_here = (d_middle * mod_here[2]).astype(bf16)
    d_branch = gather_wide(d_branch_here, "col")
    d_attended = matmul(d_branch, w_out_here, 1, 1).astype(bf16).reshape(SEQ, heads_here, HD)
    d_w_out = grad_sum(in_blocks(matmul(attended, d_branch, 0, 0), rows))
    d_out_bias = jnp.sum(d_branch_here.astype(f32), axis=0)

    early = jnp.stack(
        [
            jnp.sum(d_middle * branch_here, axis=0),
            jnp.sum(d_input2, axis=0),
            jnp.sum(d_input2 * normed2_here, axis=0),
            jnp.sum(dy_block * feed, axis=0),
            d_out_bias,
            d_fc2_bias,
        ]
    )

    d_qkv = attend_back(queries, keys, values, log_totals, d_attended)
    d_input1 = matmul(d_qkv, w_qkv_all, 1, 1)
    sums1 = norm_sums(d_input1, mod[1], normed1)
    d_input1 = sum_scatter(in_blocks(d_input1, cols), "col")
    d_w_qkv = grad_sum(matmul(input1, d_qkv, 0, 0).reshape(rows, width, 3 * width))
    d_w_qkv = d_w_qkv.reshape(width, 3, width)
    d_qkv_sums = jnp.sum(d_qkv.astype(f32), axis=0).reshape(3, width)
    d_tokens = d_middle + norm_back(d_input1, mod_here[1], normed1_here, inv1, sums1)
    d_tokens = transposed(d_tokens.astype(bf16)).astype(f32)

    late = jnp.stack([jnp.sum(d_input1, axis=0), jnp.sum(d_input1 * normed1_here, axis=0)])

    def every_latent(part):
        full = lax.all_gather(part, ("dp", "row", "col"), axis=0)
        full = full.reshape(-1, cols, part.shape[0], width)
        return lax.dynamic_index_in_dim(full, row, 1, keepdims=False)

    early, late = every_latent(early), every_latent(late)
    d_out_bias = jnp.sum(early[:, 4], axis=0)
    d_fc2_bias = jnp.sum(early[:, 5], axis=0)
    d_mod = jnp.concatenate([late, early[:, :4]], axis=1)
    d_ada_bias = jnp.sum(d_mod, axis=0)
    all_ids = lax.all_gather(jnp.stack([class_ids, time_ids]), "dp", axis=1, tiled=True)
    onehot, condition = embed(all_ids[0], all_ids[1])
    activated = jax.nn.silu(condition).astype(bf16).astype(f32)
    d_ada_weight = jnp.einsum("qk,qfb->kfb", activated, d_mod, precision=highest)
    d_activated = jnp.einsum(
        "qnp,unp->qu", d_mod, adaptive_norm_weight.astype(f32), precision=highest
    )
    d_activated = lax.psum(d_activated, "row")
    d_condition = jax.vjp(jax.nn.silu, condition)[1](d_activated)[0]
    d_table = lax.dot_general(
        onehot.astype(f32), d_condition, (((0,), (0,)), ((), ())), precision=highest
    )
    bias_sums = lax.psum(
        jnp.concatenate([d_fc1_bias, d_qkv_sums[0], d_qkv_sums[2]]), ("dp", "row")
    )
    d_fc1_bias = bias_sums[: d_fc1_bias.shape[0]]
    d_query_value_bias = bias_sums[d_fc1_bias.shape[0] :].reshape(2, width)
    return (
        mixed,
        d_tokens,
        d_table,
        d_ada_weight,
        d_ada_bias,
        d_w_qkv,
        d_query_value_bias,
        d_w_out,
        d_out_bias,
        d_w_fc1,
        d_fc1_bias,
        d_w_fc2,
        d_fc2_bias,
    )


def solution(mesh):
    return jax.shard_map(
        per_device,
        mesh=mesh,
        in_specs=(
            P(("dp", "col"), "row"),
            P("dp"),
            P("dp"),
            P(None, "col"),
            P("col", None, "row"),
            P(None, "row"),
            P("row", None, "col"),
            P(None, "col"),
            P("col", "row"),
            P("row"),
            P("row", "col"),
            P("col"),
            P("col", "row"),
            P("row"),
            P(("dp", "col"), "row"),
        ),
        out_specs=(
            P(("dp", "col"), "row"),
            P(("dp", "col"), "row"),
            P(None, "col"),
            P("col", None, "row"),
            P(None, "row"),
            P("row", None, "col"),
            P(None, "col"),
            P("col", "row"),
            P("row"),
            P("row", "col"),
            P("col"),
            P("col", "row"),
            P("row"),
        ),
        check_vma=False,
    )
```
